32 devices in a mesh: ctx: 8 (over y, x, core), tp: 4 (over z).
Axes of the slice: x: 2, y: 2, z: 4, core: 2. Of those that a mesh axis runs over, the one named last changes fastest.
Arguments:
- qkv_first: bfloat16 [3, 8192, 4096], P(None, 'ctx', 'tp'), may hold values from -6 to 6
- short_first: float32 [3, 3, 4096], P(None, None, 'tp'), may hold values from -4 to 4
- medium_filter: bfloat16 [4096, 128], P('tp'), may hold values from -0.5 to 0.5
- out_weight: bfloat16 [4096, 4096], P('tp', 'ctx'), may hold values from -0.09375 to 0.09375
- residual_in: bfloat16 [8192, 4096], P('ctx', 'tp'), may hold values from -64 to 64
- norm_gain: bfloat16 [4096], P('tp'), may hold values from 0.5 to 1.5
- in_weight: bfloat16 [3, 4096, 4096], P(None, 'ctx', 'tp'), may hold values from -0.09375 to 0.09375
- short_second: float32 [3, 3, 4096], P(None, None, 'tp'), may hold values from -4 to 4
- rates: float32 [16, 4096], P(None, 'tp'), as said below
- residues: float32 [16, 4096], P(None, 'tp'), may hold values from -0.024 to 0.024
- skip_gain: float32 [4096], P('tp'), may hold values from -4 to 4
Outputs:
- hidden: bfloat16 [8192, 4096], P('ctx', 'tp')
- mixed: bfloat16 [8192, 4096], P('ctx', 'tp')
The draws below stay inside these ranges and needn't reach their ends.
Inputs may be any that keep to these rules, and one draw needn't show every extreme that they name: `rates`: each entry is a positive decay rate per token, between 1e-7 and 0.05.
All inputs are finite; a program needn't handle non-finite values.
Results may differ from the reference program's by a relative error of at most 0.025.
Values may be sent and summed in bfloat16 or wider, within the bound.
A program may use at most 128 MiB of HBM per device.

```python
import math
import jax
import jax.numpy as jnp
from jax import lax

D = 4096
POLES = 16
TAPS = 128
SHORT = 3
TOKENS = 8192
N_TP = 4


def draw_residual_in(key, part):
    row_key = jax.random.fold_in(key, 11)
    entry_key = jax.random.fold_in(key, 12)
    columns = jnp.arange(D, dtype=jnp.float32) / D
    column_scale = 10.0 ** (columns - 0.5)
    row_scale = jnp.exp(jax.random.uniform(row_key, (TOKENS, 1), jnp.float32, math.log(0.3), math.log(3.0)))
    values = jnp.clip(jax.random.normal(entry_key, (TOKENS, D), jnp.float32), -6.0, 6.0)
    return (values * row_scale * column_scale[None, :]).astype(jnp.bfloat16)


def draw_rates(key, part):
    level_key = jax.random.fold_in(key, 22)
    levels = jax.random.uniform(level_key, (POLES, D), jnp.float32)
    lower_log = math.log(1e-07)
    upper_log = jnp.full((POLES, D), math.log(0.05), jnp.float32)
    return jnp.exp(lower_log + levels * (upper_log - lower_log)).astype(jnp.float32)


def block_levels(rng, dims, cuts, low, top_value):
    loudness = 1.0
    for dim, blocks in cuts:
        steps = jax.random.uniform(jax.random.fold_in(jax.random.fold_in(rng, 6), dim), (blocks,), jnp.float32, low / len(cuts), top_value / len(cuts))
        loudness = loudness * jnp.repeat(jnp.exp(steps), dims[dim] // blocks).reshape((-1,) + (1,) * (len(dims) - 1 - dim))
    return loudness


def gaussian(key, dims, deviation, most, cuts=(), held_as=jnp.bfloat16):
    factor_of = block_levels(key, dims, cuts, -0.22, 0.18) if cuts else 1.0
    array = jax.random.normal(key, dims, jnp.float32) * deviation * factor_of
    return jnp.minimum(jnp.maximum(array, -most), most).astype(held_as)


def setup_inputs(seed: int = 0) -> dict:
    arg_keys = jax.random.split(jax.random.key(seed), 12)
    return {
        "qkv_first": gaussian(arg_keys[0], (3, TOKENS, D), 1.0, 6.0, ((1, 8), (2, 4))),
        "short_first": gaussian(arg_keys[1], (3, SHORT, D), 0.6, 4.0, ((2, 4),), jnp.float32),
        "medium_filter": gaussian(arg_keys[2], (D, TAPS), TAPS ** -0.5, 0.5, ((0, 4),)),
        "out_weight": gaussian(arg_keys[3], (D, D), D ** -0.5, 0.09375, ((0, 4), (1, 8))),
        "residual_in": draw_residual_in(jax.random.fold_in(arg_keys[11], 71), 0),
        "norm_gain": jnp.clip(1.0 + 0.1 * jax.random.normal(arg_keys[5], (D,), jnp.float32), 0.5, 1.5).astype(jnp.bfloat16),
        "in_weight": gaussian(arg_keys[6], (3, D, D), D ** -0.5, 0.09375, ((1, 8), (2, 4))),
        "short_second": gaussian(arg_keys[7], (3, SHORT, D), 0.6, 4.0, ((2, 4),), jnp.float32),
        "rates": draw_rates(jax.random.fold_in(arg_keys[11], 71), 0),
        "residues": gaussian(arg_keys[9], (POLES, D), 0.004, 0.024, ((1, 4),), jnp.float32),
        "skip_gain": gaussian(arg_keys[10], (D,), 1.0, 4.0, ((0, 4),), jnp.float32),
    }


EPSILON = 1e-05

def featurize(extended, tap_weights):
    widened = extended.astype(jnp.float32)
    return tap_weights[:, 0][:, None, :] * widened[:, 2:] + tap_weights[:, 1][:, None, :] * widened[:, 1:-1] + tap_weights[:, 2][:, None, :] * widened[:, :-2]

def medium_reference(gated, filters):
    length = gated.shape[0]
    padded = jnp.pad(gated.astype(jnp.float32), ((TAPS - 1, 0), (0, 0)))
    filter_values = filters.astype(jnp.float32)

    def add_tap(lag_index, totals):
        shifted = lax.dynamic_slice_in_dim(padded, (TAPS - 1 - lag_index).astype(jnp.int32), length, 0)
        column = lax.dynamic_slice_in_dim(filter_values, lag_index.astype(jnp.int32), 1, 1)[:, 0]
        return totals + shifted * column
    return lax.fori_loop(0, TAPS, add_tap, jnp.zeros(gated.shape, jnp.float32))

def modal_reference(gated, rates, residues):
    inputs = gated.astype(jnp.float32)
    poles = jnp.exp(-rates)

    def advance(state, row_input):
        state = poles * state + row_input[None, :]
        return (state, lax.optimization_barrier(jnp.sum(residues * state, axis=0)))
    _, outputs = lax.scan(advance, jnp.zeros(rates.shape, jnp.float32), inputs)
    return outputs

def reference(qkv_first, short_first, medium_filter, out_weight, residual_in, norm_gain, in_weight, short_second, rates, residues, skip_gain):
    padded_first = jnp.pad(qkv_first, ((0, 0), (2, 0), (0, 0)))
    features = featurize(padded_first, short_first)
    gated_first = (features[1] * features[2]).astype(jnp.bfloat16)
    mixed_first = (features[0] * medium_reference(gated_first, medium_filter)).astype(jnp.bfloat16)
    channels = D // N_TP
    summed = jnp.zeros(residual_in.shape, jnp.float32)
    for group_index in range(N_TP):
        lower = group_index * channels
        partial_value = jnp.dot(mixed_first[:, lower:lower + channels], out_weight[lower:lower + channels], preferred_element_type=jnp.float32)
        summed = summed + lax.optimization_barrier(partial_value.astype(jnp.bfloat16)).astype(jnp.float32)
    hidden = (residual_in.astype(jnp.float32) + summed).astype(jnp.bfloat16)
    hidden_values = hidden.astype(jnp.float32)
    mean_square = lax.optimization_barrier(jnp.sum(hidden_values * hidden_values, axis=1)) / D
    normed = (hidden_values * lax.rsqrt(mean_square + EPSILON)[:, None] * norm_gain.astype(jnp.float32)).astype(jnp.bfloat16)
    qkv_second = jnp.stack([jnp.dot(normed, in_weight[which], preferred_element_type=jnp.float32).astype(jnp.bfloat16) for which in range(3)])
    padded_second = jnp.pad(qkv_second, ((0, 0), (2, 0), (0, 0)))
    features_second = featurize(padded_second, short_second)
    gated_second = (features_second[1] * features_second[2]).astype(jnp.bfloat16)
    modal = modal_reference(gated_second, rates, residues)
    mixed = (features_second[0] * (modal + skip_gain * gated_second.astype(jnp.float32))).astype(jnp.bfloat16)
    return (hidden, mixed)
```

```python
import functools
import math

import jax
import jax.numpy as jnp
from jax import lax
from jax.experimental import pallas as pl
from jax.experimental.pallas import tpu as pltpu
from jax.sharding import PartitionSpec as P

EPSILON = 1e-05
LANES = 128
BF = jnp.bfloat16
F32 = jnp.float32


def shifted(x, axis, by):
    size = lax.axis_size(axis)
    pairs = [(i, i + by) for i in range(size) if 0 <= i + by < size]
    return lax.ppermute(x, axis, pairs)


def to_rows(x):
    return x.reshape(-1, LANES)


def spread(x_ref, rows, channels, block, first, which):
    groups = channels // LANES
    for m in which:
        for g in range(groups):
            rows[m, pl.ds(first * groups + g, block, groups), :] = x_ref[
                m, :, g * LANES : (g + 1) * LANES
            ].astype(F32)


def collect(out_ref, rows, channels, block):
    groups = channels // LANES
    for g in range(groups):
        out_ref[:, g * LANES : (g + 1) * LANES] = rows[pl.ds(g, block, groups), :].astype(BF)


def slab(ref, token, groups):
    return ref[pl.ds(pl.multiple_of(token * groups, groups), groups), :]


def fir_kernel(
    taps, unit, x_ref, xin_ref, gin_ref, w_ref, f_ref, out_ref, xout_ref, gout_ref, rows, gated, result
):
    block, channels = out_ref.shape
    groups = channels // LANES
    step = pl.program_id(0)

    @pl.when(step == 0)
    def _():
        for m in range(3):
            rows[m, : 2 * groups] = xin_ref[m]
        gated[: taps * groups] = gin_ref[...]

    @pl.when(step > 0)
    def _():
        for m in range(3):
            rows[m, : 2 * groups] = rows[m, block * groups : (block + 2) * groups]
        gated[: taps * groups] = gated[block * groups : (block + taps) * groups]

    spread(x_ref, rows, channels, block, 2, (0, 1, 2))

    def feature(m, token):
        total = None
        for j in range(3):
            start = pl.multiple_of((token + 2 - j) * groups, groups)
            term = w_ref[(3 * m + j) * groups : (3 * m + j + 1) * groups] * rows[m, pl.ds(start, groups), :]
            total = term if total is None else total + term
        return total

    def gate(i, carry):
        for u in range(8):
            token = i * 8 + u
            value = (feature(1, token) * feature(2, token)).astype(BF).astype(F32)
            gated[pl.ds(pl.multiple_of((token + taps) * groups, groups), groups), :] = value
        return carry

    lax.fori_loop(0, block // 8, gate, 0)

    span = 32

    def outputs(i, carry):
        base = i * unit

        def some_taps(part, totals):
            totals = list(totals)
            first = base + taps - part * span
            window = [slab(gated, first + u, groups) for u in range(unit)]
            for j in range(span):
                weight = slab(f_ref, part * span + j, groups)
                for u in range(unit):
                    totals[u] = totals[u] + weight * window[u]
                if j + 1 < span:
                    window = [slab(gated, first - j - 1, groups)] + window[:-1]
            return tuple(totals)

        zero = jnp.zeros((groups, LANES), F32)
        totals = lax.fori_loop(0, taps // span, some_taps, (zero,) * unit)
        for u in range(unit):
            token = base + u
            result[pl.ds(pl.multiple_of(token * groups, groups), groups), :] = (
                feature(0, token) * totals[u]
            )
        return carry

    lax.fori_loop(0, block // unit, outputs, 0)
    collect(out_ref, result, channels, block)

    @pl.when(step == pl.num_programs(0) - 1)
    def _():
        for m in range(3):
            xout_ref[m] = rows[m, block * groups : (block + 2) * groups]
        gout_ref[...] = gated[block * groups : (block + taps) * groups]


def fir(qkv, xin, gin, weights, filters, first, length, block):
    channels = qkv.shape[2]
    groups = channels // LANES
    taps = filters.shape[0] // groups
    offset = first // block
    return pl.pallas_call(
        functools.partial(fir_kernel, taps, 16),
        grid=(length // block,),
        in_specs=[
            pl.BlockSpec((3, block, channels), lambda i: (0, i + offset, 0)),
            pl.BlockSpec(xin.shape, lambda i: (0, 0, 0)),
            pl.BlockSpec(gin.shape, lambda i: (0, 0)),
            pl.BlockSpec(weights.shape, lambda i: (0, 0)),
            pl.BlockSpec(filters.shape, lambda i: (0, 0)),
        ],
        out_specs=[
            pl.BlockSpec((block, channels), lambda i: (i, 0)),
            pl.BlockSpec(xin.shape, lambda i: (0, 0, 0)),
            pl.BlockSpec(gin.shape, lambda i: (0, 0)),
        ],
        out_shape=[
            jax.ShapeDtypeStruct((length, channels), BF),
            jax.ShapeDtypeStruct(xin.shape, F32),
            jax.ShapeDtypeStruct(gin.shape, F32),
        ],
        scratch_shapes=[
            pltpu.VMEM((3, (block + 2) * groups, LANES), F32),
            pltpu.VMEM(((block + taps) * groups, LANES), F32),
            pltpu.VMEM((block * groups, LANES), F32),
        ],
        compiler_params=pltpu.CompilerParams(vmem_limit_bytes=24 * 2**20),
        cost_estimate=pl.CostEstimate(
            flops=2 * taps * length * channels, bytes_accessed=8 * length * channels, transcendentals=0
        ),
        name="medium_filter",
    )(qkv, xin, gin, weights, filters)


def modal_kernel(poles, finish, x_ref, xin_ref, w_ref, p_ref, r_ref, s_ref, d_ref, out_ref, rows, state, result):
    block, channels = x_ref.shape[1:]
    groups = channels // LANES
    step = pl.program_id(0)
    which = (0, 1, 2) if finish else (1, 2)

    @pl.when(step == 0)
    def _():
        for m in which:
            rows[m, : 2 * groups] = xin_ref[m]
        state[...] = s_ref[...]

    @pl.when(step > 0)
    def _():
        for m in which:
            rows[m, : 2 * groups] = rows[m, block * groups : (block + 2) * groups]

    spread(x_ref, rows, channels, block, 2, which)

    def feature(m, token):
        total = None
        for j in range(3):
            start = pl.multiple_of((token + 2 - j) * groups, groups)
            term = w_ref[(3 * m + j) * groups : (3 * m + j + 1) * groups] * rows[m, pl.ds(start, groups), :]
            total = term if total is None else total + term
        return total

    def tokens(i, states):
        states = list(states)
        for u in range(8):
            token = i * 8 + u
            value = (feature(1, token) * feature(2, token)).astype(BF).astype(F32)
            sums = [d_ref[...] * value] if finish else []
            for n in range(poles):
                at = slice(n * groups, (n + 1) * groups)
                states[n] = p_ref[at] * states[n] + value
                if finish:
                    term = r_ref[at] * states[n]
                    if n < 3:
                        sums.append(term)
                    else:
                        sums[n % 4] = sums[n % 4] + term
            if finish:
                result[pl.ds(pl.multiple_of(token * groups, groups), groups), :] = feature(0, token) * (
                    (sums[0] + sums[1]) + (sums[2] + sums[3])
                )
        return tuple(states)

    held = tuple(state[n * groups : (n + 1) * groups] for n in range(poles))
    held = lax.fori_loop(0, block // 8, tokens, held)
    for n in range(poles):
        state[n * groups : (n + 1) * groups] = held[n]
    if finish:
        collect(out_ref, result, channels, block)
    else:

        @pl.when(step == pl.num_programs(0) - 1)
        def _():
            out_ref[...] = state[...]


def modal(qkv, xin, weights, decay, residues, state, skip, block, finish):
    _, length, channels = qkv.shape
    groups = channels // LANES
    poles = decay.shape[0] // groups

    def whole(a):
        return pl.BlockSpec(a.shape, lambda i: (0,) * a.ndim)

    if finish:
        out_spec = pl.BlockSpec((block, channels), lambda i: (i, 0))
        out_shape = jax.ShapeDtypeStruct((length, channels), BF)
    else:
        out_spec = whole(state)
        out_shape = jax.ShapeDtypeStruct(state.shape, F32)
    return pl.pallas_call(
        functools.partial(modal_kernel, poles, finish),
        grid=(length // block,),
        in_specs=[pl.BlockSpec((3, block, channels), lambda i: (0, i, 0))]
        + [whole(a) for a in (xin, weights, decay, residues, state, skip)],
        out_specs=out_spec,
        out_shape=out_shape,
        scratch_shapes=[
            pltpu.VMEM((3, (block + 2) * groups, LANES), F32),
            pltpu.VMEM(state.shape, F32),
            pltpu.VMEM((block * groups, LANES), F32),
        ],
        compiler_params=pltpu.CompilerParams(vmem_limit_bytes=24 * 2**20),
        cost_estimate=pl.CostEstimate(
            flops=4 * poles * length * channels, bytes_accessed=8 * length * channels, transcendentals=0
        ),
        name="modal_finish" if finish else "modal_ends",
    )(qkv, xin, weights, decay, residues, state, skip)


def gate_tail(qkv, weights, count):
    length = qkv.shape[1]
    wide = qkv[1:, length - count - 2 :].astype(F32)
    features = (
        weights[1:, 0][:, None] * wide[:, 2:]
        + weights[1:, 1][:, None] * wide[:, 1:-1]
        + weights[1:, 2][:, None] * wide[:, :-2]
    )
    return (features[0] * features[1]).astype(BF)


def on_device(
    chunk_count,
    qkv_first,
    short_first,
    medium_filter,
    out_weight,
    residual_in,
    norm_gain,
    in_weight,
    short_second,
    rates,
    residues,
    skip_gain,
):
    _, length, channels = qkv_first.shape
    taps = medium_filter.shape[1]
    width = channels * lax.axis_size("tp")
    block = math.gcd(length // chunk_count, 128)

    rim = shifted(qkv_first[:, length - 2 :], "ctx", 1)
    gated_rim = shifted(gate_tail(qkv_first, short_first, taps), "ctx", 1)
    out_all = lax.all_gather(out_weight, "ctx", axis=1, tiled=True)
    in_all = lax.all_gather(in_weight, "ctx", axis=1, tiled=True)
    gain_all = lax.all_gather(norm_gain, "tp", axis=0, tiled=True).astype(F32)

    x_tail = rim.astype(F32).reshape(3, -1, LANES)
    g_tail = to_rows(gated_rim.astype(F32))
    first_taps = to_rows(short_first)
    filter_rows = to_rows(medium_filter.astype(F32).T)

    part = length // chunk_count
    hidden_parts, second_parts = [], []
    for c in range(chunk_count):
        mixed_first, x_tail, g_tail = fir(
            qkv_first, x_tail, g_tail, first_taps, filter_rows, c * part, part, block
        )
        partial_value = jnp.dot(mixed_first, out_all, preferred_element_type=F32).astype(BF)
        summed = lax.psum_scatter(partial_value, "tp", scatter_dimension=1, tiled=True)
        residual = residual_in[c * part : (c + 1) * part]
        hidden = (residual.astype(F32) + summed.astype(F32)).astype(BF)
        hidden_parts.append(hidden)
        hidden_values = lax.all_gather(hidden, "tp", axis=1, tiled=True).astype(F32)
        squares = jnp.sum(hidden_values * hidden_values, axis=1)
        inverse_rms = lax.rsqrt(squares / width + EPSILON)
        normed = (hidden_values * inverse_rms[:, None] * gain_all).astype(BF)
        second_parts.append(
            jnp.einsum("tr,krc->ktc", normed, in_all, preferred_element_type=F32).astype(BF)
        )
    hidden = jnp.concatenate(hidden_parts, axis=0)
    qkv_second = jnp.concatenate(second_parts, axis=1)

    second_rim = shifted(qkv_second[:, length - 2 :], "ctx", 1).astype(F32).reshape(3, -1, LANES)
    second_taps = to_rows(short_second)
    decay = to_rows(jnp.exp(-rates))
    residue_rows = to_rows(residues)
    skip = to_rows(skip_gain)
    step_block = math.gcd(length, 256)
    ends = modal(
        qkv_second, second_rim, second_taps, decay, residue_rows, jnp.zeros_like(decay), skip, step_block, False
    )
    place = lax.axis_index("ctx")
    ends_all = lax.all_gather(ends, "ctx")
    laps = place - 1 - jnp.arange(lax.axis_size("ctx"), dtype=jnp.int32)
    passed = jnp.exp(-to_rows(rates)[None] * (jnp.maximum(laps, 0) * length).astype(F32)[:, None, None])
    state_in = jnp.sum(jnp.where((laps >= 0)[:, None, None], passed * ends_all, 0.0), axis=0)
    mixed = modal(
        qkv_second, second_rim, second_taps, decay, residue_rows, state_in, skip, step_block, True
    )
    return (hidden, mixed)


def solution(mesh):
    placed = (
        P(None, "ctx", "tp"),
        P(None, None, "tp"),
        P("tp", None),
        P("tp", "ctx"),
        P("ctx", "tp"),
        P("tp"),
        P(None, "ctx", "tp"),
        P(None, None, "tp"),
        P(None, "tp"),
        P(None, "tp"),
        P("tp"),
    )
    return jax.shard_map(
        functools.partial(on_device, 4),
        mesh=mesh,
        in_specs=placed,
        out_specs=(P("ctx", "tp"), P("ctx", "tp")),
        check_vma=False,
    )
```

```python
import functools
import math

import jax
import jax.numpy as jnp
from jax import lax
from jax.experimental import pallas as pl
from jax.experimental.pallas import tpu as pltpu
from jax.sharding import PartitionSpec as P

EPSILON = 1e-05
LANES = 128
BF = jnp.bfloat16
F32 = jnp.float32


def shifted(x, axis, by):
    size = lax.axis_size(axis)
    pairs = [(i, i + by) for i in range(size) if 0 <= i + by < size]
    return lax.ppermute(x, axis, pairs)


def gather_rows(x, axis, ahead):
    size = lax.axis_size(axis)
    count = size.bit_length() - 1
    if size != 1 << count:
        return lax.all_gather(x, axis, axis=1, tiled=True)
    place = lax.axis_index(axis)
    order = [b for b in ahead if b < count] + [b for b in range(count - 1, -1, -1) if b not in ahead]
    held = x.reshape(x.shape[:1] + (1,) * count + x.shape[1:])
    for b in order:
        other = lax.ppermute(held, axis, [(i, i ^ (1 << b)) for i in range(size)])
        upper = (place >> b) & 1 == 1
        low, high = jnp.where(upper, other, held), jnp.where(upper, held, other)
        held = jnp.concatenate([low, high], axis=count - b)
    return held.reshape(x.shape[0], -1, x.shape[2])


def to_rows(x):
    return x.reshape(-1, LANES)


def spread(x_ref, rows, channels, block, first, which):
    groups = channels // LANES
    for m in which:
        for g in range(groups):
            rows[m, pl.ds(first * groups + g, block, groups), :] = x_ref[
                m, :, g * LANES : (g + 1) * LANES
            ].astype(F32)


def collect(out_ref, rows, channels, block):
    groups = channels // LANES
    for g in range(groups):
        out_ref[:, g * LANES : (g + 1) * LANES] = rows[pl.ds(g, block, groups), :].astype(BF)


def slab(ref, token, groups):
    return ref[pl.ds(pl.multiple_of(token * groups, groups), groups), :]


def fir_kernel(
    taps, unit, x_ref, xin_ref, gin_ref, w_ref, f_ref, out_ref, xout_ref, gout_ref, rows, gated, result
):
    block, channels = out_ref.shape
    groups = channels // LANES
    step = pl.program_id(0)

    @pl.when(step == 0)
    def _():
        for m in range(3):
            rows[m, : 2 * groups] = xin_ref[m]
        gated[: taps * groups] = gin_ref[...]

    @pl.when(step > 0)
    def _():
        for m in range(3):
            rows[m, : 2 * groups] = rows[m, block * groups : (block + 2) * groups]
        gated[: taps * groups] = gated[block * groups : (block + taps) * groups]

    spread(x_ref, rows, channels, block, 2, (0, 1, 2))

    def feature(m, token):
        total = None
        for j in range(3):
            start = pl.multiple_of((token + 2 - j) * groups, groups)
            term = w_ref[(3 * m + j) * groups : (3 * m + j + 1) * groups] * rows[m, pl.ds(start, groups), :]
            total = term if total is None else total + term
        return total

    def gate(i, carry):
        for u in range(8):
            token = i * 8 + u
            value = (feature(1, token) * feature(2, token)).astype(BF).astype(F32)
            gated[pl.ds(pl.multiple_of((token + taps) * groups, groups), groups), :] = value
        return carry

    lax.fori_loop(0, block // 8, gate, 0)

    span = 32

    def outputs(i, carry):
        base = i * unit

        def some_taps(part, totals):
            totals = list(totals)
            first = base + taps - part * span
            window = [slab(gated, first + u, groups) for u in range(unit)]
            for j in range(span):
                weight = slab(f_ref, part * span + j, groups)
                for u in range(unit):
                    totals[u] = totals[u] + weight * window[u]
                if j + 1 < span:
                    window = [slab(gated, first - j - 1, groups)] + window[:-1]
            return tuple(totals)

        zero = jnp.zeros((groups, LANES), F32)
        totals = lax.fori_loop(0, taps // span, some_taps, (zero,) * unit)
        for u in range(unit):
            token = base + u
            result[pl.ds(pl.multiple_of(token * groups, groups), groups), :] = (
                feature(0, token) * totals[u]
            )
        return carry

    lax.fori_loop(0, block // unit, outputs, 0)
    collect(out_ref, result, channels, block)

    @pl.when(step == pl.num_programs(0) - 1)
    def _():
        for m in range(3):
            xout_ref[m] = rows[m, block * groups : (block + 2) * groups]
        gout_ref[...] = gated[block * groups : (block + taps) * groups]


def fir(qkv, xin, gin, weights, filters, first, length, block):
    channels = qkv.shape[2]
    groups = channels // LANES
    taps = filters.shape[0] // groups
    offset = first // block
    return pl.pallas_call(
        functools.partial(fir_kernel, taps, 16),
        grid=(length // block,),
        in_specs=[
            pl.BlockSpec((3, block, channels), lambda i: (0, i + offset, 0)),
            pl.BlockSpec(xin.shape, lambda i: (0, 0, 0)),
            pl.BlockSpec(gin.shape, lambda i: (0, 0)),
            pl.BlockSpec(weights.shape, lambda i: (0, 0)),
            pl.BlockSpec(filters.shape, lambda i: (0, 0)),
        ],
        out_specs=[
            pl.BlockSpec((block, channels), lambda i: (i, 0)),
            pl.BlockSpec(xin.shape, lambda i: (0, 0, 0)),
            pl.BlockSpec(gin.shape, lambda i: (0, 0)),
        ],
        out_shape=[
            jax.ShapeDtypeStruct((length, channels), BF),
            jax.ShapeDtypeStruct(xin.shape, F32),
            jax.ShapeDtypeStruct(gin.shape, F32),
        ],
        scratch_shapes=[
            pltpu.VMEM((3, (block + 2) * groups, LANES), F32),
            pltpu.VMEM(((block + taps) * groups, LANES), F32),
            pltpu.VMEM((block * groups, LANES), F32),
        ],
        compiler_params=pltpu.CompilerParams(vmem_limit_bytes=24 * 2**20),
        cost_estimate=pl.CostEstimate(
            flops=2 * taps * length * channels, bytes_accessed=8 * length * channels, transcendentals=0
        ),
        name="medium_filter",
    )(qkv, xin, gin, weights, filters)


def modal_kernel(poles, finish, x_ref, xin_ref, w_ref, p_ref, r_ref, s_ref, d_ref, out_ref, rows, state, result):
    block, channels = x_ref.shape[1:]
    groups = channels // LANES
    step = pl.program_id(0)
    which = (0, 1, 2) if finish else (1, 2)

    @pl.when(step == 0)
    def _():
        for m in which:
            rows[m, : 2 * groups] = xin_ref[m]
        state[...] = s_ref[...]

    @pl.when(step > 0)
    def _():
        for m in which:
            rows[m, : 2 * groups] = rows[m, block * groups : (block + 2) * groups]

    spread(x_ref, rows, channels, block, 2, which)

    def feature(m, token):
        total = None
        for j in range(3):
            start = pl.multiple_of((token + 2 - j) * groups, groups)
            term = w_ref[(3 * m + j) * groups : (3 * m + j + 1) * groups] * rows[m, pl.ds(start, groups), :]
            total = term if total is None else total + term
        return total

    def tokens(i, states):
        states = list(states)
        for u in range(8):
            token = i * 8 + u
            value = (feature(1, token) * feature(2, token)).astype(BF).astype(F32)
            sums = [d_ref[...] * value] if finish else []
            for n in range(poles):
                at = slice(n * groups, (n + 1) * groups)
                states[n] = p_ref[at] * states[n] + value
                if finish:
                    term = r_ref[at] * states[n]
                    if n < 3:
                        sums.append(term)
                    else:
                        sums[n % 4] = sums[n % 4] + term
            if finish:
                result[pl.ds(pl.multiple_of(token * groups, groups), groups), :] = feature(0, token) * (
                    (sums[0] + sums[1]) + (sums[2] + sums[3])
                )
        return tuple(states)

    held = tuple(state[n * groups : (n + 1) * groups] for n in range(poles))
    held = lax.fori_loop(0, block // 8, tokens, held)
    for n in range(poles):
        state[n * groups : (n + 1) * groups] = held[n]
    if finish:
        collect(out_ref, result, channels, block)
    else:

        @pl.when(step == pl.num_programs(0) - 1)
        def _():
            out_ref[...] = state[...]


def modal(qkv, xin, weights, decay, residues, state, skip, block, finish):
    _, length, channels = qkv.shape
    groups = channels // LANES
    poles = decay.shape[0] // groups

    def whole(a):
        return pl.BlockSpec(a.shape, lambda i: (0,) * a.ndim)

    if finish:
        out_spec = pl.BlockSpec((block, channels), lambda i: (i, 0))
        out_shape = jax.ShapeDtypeStruct((length, channels), BF)
    else:
        out_spec = whole(state)
        out_shape = jax.ShapeDtypeStruct(state.shape, F32)
    return pl.pallas_call(
        functools.partial(modal_kernel, poles, finish),
        grid=(length // block,),
        in_specs=[pl.BlockSpec((3, block, channels), lambda i: (0, i, 0))]
        + [whole(a) for a in (xin, weights, decay, residues, state, skip)],
        out_specs=out_spec,
        out_shape=out_shape,
        scratch_shapes=[
            pltpu.VMEM((3, (block + 2) * groups, LANES), F32),
            pltpu.VMEM(state.shape, F32),
            pltpu.VMEM((block * groups, LANES), F32),
        ],
        compiler_params=pltpu.CompilerParams(vmem_limit_bytes=24 * 2**20),
        cost_estimate=pl.CostEstimate(
            flops=4 * poles * length * channels, bytes_accessed=8 * length * channels, transcendentals=0
        ),
        name="modal_finish" if finish else "modal_ends",
    )(qkv, xin, weights, decay, residues, state, skip)


def gate_tail(qkv, weights, count):
    length = qkv.shape[1]
    wide = qkv[1:, length - count - 2 :].astype(F32)
    features = (
        weights[1:, 0][:, None] * wide[:, 2:]
        + weights[1:, 1][:, None] * wide[:, 1:-1]
        + weights[1:, 2][:, None] * wide[:, :-2]
    )
    return (features[0] * features[1]).astype(BF)


def on_device(
    chunk_count,
    qkv_first,
    short_first,
    medium_filter,
    out_weight,
    residual_in,
    norm_gain,
    in_weight,
    short_second,
    rates,
    residues,
    skip_gain,
):
    _, length, channels = qkv_first.shape
    taps = medium_filter.shape[1]
    width = channels * lax.axis_size("tp")
    block = math.gcd(length // chunk_count, 128)

    rim = shifted(qkv_first[:, length - 2 :], "ctx", 1)
    gated_rim = shifted(gate_tail(qkv_first, short_first, taps), "ctx", 1)
    out_all = lax.all_gather(out_weight, "ctx", axis=1, tiled=True)
    in_weight, out_all = lax.optimization_barrier((in_weight, out_all))
    half = channels // 2
    in_halves = (
        gather_rows(in_weight[:, :, :half], "ctx", (1, 2)),
        gather_rows(in_weight[:, :, half:], "ctx", (2, 1)),
    )
    gain_all = lax.all_gather(norm_gain, "tp", axis=0, tiled=True).astype(F32)

    x_tail = rim.astype(F32).reshape(3, -1, LANES)
    g_tail = to_rows(gated_rim.astype(F32))
    first_taps = to_rows(short_first)
    filter_rows = to_rows(medium_filter.astype(F32).T)

    part = length // chunk_count
    hidden_parts, second_parts = [], []
    for c in range(chunk_count):
        mixed_first, x_tail, g_tail = fir(
            qkv_first, x_tail, g_tail, first_taps, filter_rows, c * part, part, block
        )
        partial_value = jnp.dot(mixed_first, out_all, preferred_element_type=F32).astype(BF)
        summed = lax.psum_scatter(partial_value, "tp", scatter_dimension=1, tiled=True)
        residual = residual_in[c * part : (c + 1) * part]
        hidden = (residual.astype(F32) + summed.astype(F32)).astype(BF)
        hidden_parts.append(hidden)
        hidden_values = lax.all_gather(hidden, "tp", axis=1, tiled=True).astype(F32)
        squares = jnp.sum(hidden_values * hidden_values, axis=1)
        inverse_rms = lax.rsqrt(squares / width + EPSILON)
        normed = (hidden_values * inverse_rms[:, None] * gain_all).astype(BF)
        products = [
            jnp.einsum("tr,krc->ktc", normed, w, preferred_element_type=F32).astype(BF) for w in in_halves
        ]
        second_parts.append(jnp.concatenate(products, axis=2))
    hidden = jnp.concatenate(hidden_parts, axis=0)
    qkv_second = jnp.concatenate(second_parts, axis=1)

    second_rim = shifted(qkv_second[:, length - 2 :], "ctx", 1).astype(F32).reshape(3, -1, LANES)
    second_taps = to_rows(short_second)
    decay = to_rows(jnp.exp(-rates))
    residue_rows = to_rows(residues)
    skip = to_rows(skip_gain)
    step_block = math.gcd(length, 256)
    ends = modal(
        qkv_second, second_rim, second_taps, decay, residue_rows, jnp.zeros_like(decay), skip, step_block, False
    )
    place = lax.axis_index("ctx")
    ends_all = lax.all_gather(ends, "ctx")
    laps = place - 1 - jnp.arange(lax.axis_size("ctx"), dtype=jnp.int32)
    passed = jnp.exp(-to_rows(rates)[None] * (jnp.maximum(laps, 0) * length).astype(F32)[:, None, None])
    state_in = jnp.sum(jnp.where((laps >= 0)[:, None, None], passed * ends_all, 0.0), axis=0)
    mixed = modal(
        qkv_second, second_rim, second_taps, decay, residue_rows, state_in, skip, step_block, True
    )
    return (hidden, mixed)


def solution(mesh):
    placed = (
        P(None, "ctx", "tp"),
        P(None, None, "tp"),
        P("tp", None),
        P("tp", "ctx"),
        P("ctx", "tp"),
        P("tp"),
        P(None, "ctx", "tp"),
        P(None, None, "tp"),
        P(None, "tp"),
        P(None, "tp"),
        P("tp"),
    )
    return jax.shard_map(
        functools.partial(on_device, 4),
        mesh=mesh,
        in_specs=placed,
        out_specs=(P("ctx", "tp"), P("ctx", "tp")),
        check_vma=False,
    )
```
